32 devices in a mesh: grp: 4 (over y, x), occ: 8 (over z, core).
Axes of the slice: x: 2, y: 2, z: 4, core: 2. Of those that a mesh axis runs over, the one named last changes fastest.
Arguments:
- b_ints: bfloat16 [256, 768, 256], P(('grp', 'occ')), may hold values from -6 to 6
- osv_vecs: bfloat16 [256, 768, 128], P(('grp', 'occ')), may hold values from -0.21875 to 0.21875
- inv_denom: float32 [256, 128], P(('grp', 'occ')), may hold values from 0.5 to 4
- domains: int32 [256, 6], P('grp'), may hold values from 0 to 95, all different within a row
- dom_count: int32 [256], P('grp'), may hold values from 1 to 6
- owner_slot: int32 [96], replicated, may hold values from 0 to 95, each once
Outputs:
- gamma_tiles: bfloat16 [256, 96, 128], P('occ', 'grp')
The draws below stay inside these ranges and needn't reach their ends.
Inputs may be any that keep to these rules, and one draw needn't show every extreme that they name: `domains`: each row names distinct tiles.
All inputs are finite; a program needn't handle non-finite values.
Results may differ from the reference program's by a relative error of at most 0.0056.
Values may be sent and summed in bfloat16 or wider, within the bound.
A program may use at most 64 MiB of HBM per device.

```python
import math
import jax
import jax.numpy as jnp
from jax import lax

TILE = 128
KD = 6
NOSV = 128
NT = 96
NB = 256
NOCC = 256


def plant(entries, stream_key, low, top_value):
    spot = [jax.random.randint(jax.random.fold_in(stream_key, axis), (), 0, length) for axis, length in enumerate(entries.shape)]
    longest = entries.shape.index(max(entries.shape))
    next_to = spot[:longest] + [(spot[longest] + 1) % entries.shape[longest]] + spot[longest + 1:]
    return entries.at[tuple(spot)].set(low).at[tuple(next_to)].set(top_value)


def levels(key, dims, shards, low, largest):
    gain, own = 1.0, jax.random.fold_in(key, 6)
    for position, blocks in shards:
        steps = jnp.exp(jax.random.uniform(jax.random.fold_in(own, position), (blocks,), jnp.float32, low / len(shards), largest / len(shards)))
        gain = gain * jnp.repeat(steps, dims[position] // blocks).reshape([-1 if axis == position else 1 for axis in range(len(dims))])
    return gain


def picks_of(stream_key, rows, count, top, lift):
    order = jax.random.permutation(jax.random.fold_in(stream_key, 1), count)
    boost = order
    for power in range(3):
        boost = boost * boost // count
    boost = boost * lift // count
    tickets = jax.random.randint(jax.random.fold_in(stream_key, 2), (rows, count), 0, 4096) + boost
    holders = jax.random.permutation(jax.random.fold_in(stream_key, 3), rows)[jnp.arange(count) % rows]
    tickets = jnp.where(jnp.arange(rows)[:, None] == holders[None, :], 1 << 14, tickets)
    priority = tickets * count + jnp.arange(count)
    return lax.top_k(priority.astype(jnp.int32), top)[1].astype(jnp.int32)


def bell_draw(own_key, shape, width, limit, cuts=(), kind=jnp.bfloat16):
    result = width * jax.random.normal(own_key, shape, jnp.float32)
    if cuts:
        result = result * levels(own_key, shape, cuts, -0.22, 0.18)
    return jnp.clip(result, -limit, limit).astype(kind)


def setup_inputs(seed: int = 0) -> dict:
    arg_keys = jax.random.split(jax.random.key(seed), 7)
    b_ints = bell_draw(arg_keys[0], (NOCC, KD * TILE, NB), 1.0, 6.0, ((0, 32),))
    osv_vecs = bell_draw(arg_keys[1], (NOCC, KD * TILE, NOSV), (KD * TILE) ** -0.5, 0.21875, ((0, 32),))
    inv_denom = jnp.clip(jnp.exp(math.log(4.0) - 2.0794415 * jax.random.uniform(arg_keys[2], (NOCC, NOSV), jnp.float32) ** levels(arg_keys[2], (NOCC, NOSV), ((0, 32),), -0.2, 0.2)), 0.5, 4.0)
    domains = picks_of(arg_keys[3], NOCC, NT, KD, 512)
    dom_count = plant(jax.random.randint(arg_keys[4], (NOCC,), 1, KD + 1), jax.random.fold_in(arg_keys[4], 1), 1, KD).astype(jnp.int32)
    owner_slot = jax.random.permutation(arg_keys[5], NT).astype(jnp.int32)
    return dict(b_ints=b_ints, osv_vecs=osv_vecs, inv_denom=inv_denom, domains=domains, dom_count=dom_count, owner_slot=owner_slot)


def reference(b_ints, osv_vecs, inv_denom, domains, dom_count, owner_slot):
    nocc = b_ints.shape[0]
    blocks = nocc // 32
    keep = jnp.arange(KD, dtype=jnp.int32)[None, :] < dom_count[:, None]
    slot = jnp.where(keep, owner_slot[domains], -1).astype(jnp.int32)
    rowmask = jnp.repeat(keep, TILE, axis=1).astype(jnp.float32)
    tiles_ids = jnp.arange(NT, dtype=jnp.int32)

    def step(total, index):
        start = (index * 32).astype(jnp.int32)
        block_b = lax.dynamic_slice_in_dim(b_ints, start, 32, 0).astype(jnp.float32)
        block_q = lax.dynamic_slice_in_dim(osv_vecs, start, 32, 0).astype(jnp.float32)
        block_d = lax.dynamic_slice_in_dim(inv_denom, start, 32, 0)
        block_m = lax.dynamic_slice_in_dim(rowmask, start, 32, 0)
        block_s = lax.dynamic_slice_in_dim(slot, start, 32, 0)
        hidden = jnp.einsum('ikn,ikp->inp', block_q, block_b * block_m[:, :, None])
        scaled = (hidden * block_d[:, :, None]).astype(jnp.bfloat16)
        amp = jnp.einsum('ikn,inp->pik', block_q, scaled.astype(jnp.float32))
        amp = (amp * block_m[None]).astype(jnp.bfloat16)
        inst = amp.reshape(NB, 32 * KD, TILE).astype(jnp.float32)
        onehot = (block_s.reshape(-1)[None, :] == tiles_ids[:, None]).astype(jnp.float32)
        return total + jnp.einsum('sn,pna->psa', onehot, inst), None

    total, _ = lax.scan(step, jnp.zeros((NB, NT, TILE), jnp.float32), jnp.arange(blocks, dtype=jnp.int32))
    return total.astype(jnp.bfloat16)
```

```python
import functools

import jax
import jax.numpy as jnp
from jax import lax
from jax.experimental import pallas as pl
from jax.experimental.pallas import tpu as pltpu
from jax.sharding import PartitionSpec as P

MESH = pl.DeviceIdType.MESH
F32 = jnp.float32
BF16 = jnp.bfloat16
NX, NY, NZ, NC = 2, 2, 4, 2


def general(b_ints, osv_vecs, inv_denom, domains, dom_count, owner_slot):
    own = b_ints.shape[0]
    kdom = domains.shape[1]
    tile = b_ints.shape[1] // kdom
    ntiles = owner_slot.shape[0]
    tiles_ids = jnp.arange(ntiles, dtype=jnp.int32)
    keep_all = jnp.arange(kdom, dtype=jnp.int32)[None, :] < dom_count[:, None]
    looked = jnp.sum(jnp.where(domains[:, :, None] == tiles_ids, owner_slot, 0), axis=-1)
    slot_all = jnp.where(keep_all, looked, -1)
    start = lax.axis_index("occ") * own
    keep = lax.dynamic_slice_in_dim(keep_all, start, own, 0)
    rowmask = jnp.repeat(keep, tile, axis=1).astype(BF16)
    masked = b_ints * rowmask[:, :, None]
    hidden = jnp.einsum("ikn,ikp->inp", osv_vecs, masked, preferred_element_type=F32)
    scaled = (hidden * inv_denom[:, :, None]).astype(BF16)
    amp = jnp.einsum("ikn,inp->pik", osv_vecs, scaled, preferred_element_type=F32)
    amp = (amp * rowmask[None].astype(F32)).astype(BF16)
    got = lax.all_to_all(amp, "occ", split_axis=0, concat_axis=1, tiled=True)
    inst = got.reshape(got.shape[0], -1, tile)
    onehot = (slot_all.reshape(-1)[None, :] == tiles_ids[:, None]).astype(BF16)
    partial_sum = jnp.einsum("sn,pna->psa", onehot, inst, preferred_element_type=F32)
    summed = lax.psum_scatter(partial_sum, "grp", scatter_dimension=1, tiled=True)
    return summed.astype(BF16)


def tiles_kernel(kdom, dom_ref, cnt_ref, slot_ref, b_ref, q_ref, d_ref, out_ref, acc, stage, sems):
    i = pl.program_id(0)
    own = pl.num_programs(0)
    blocks, _, cols, tile = acc.shape
    row = lax.axis_index("occ") * own + i

    @pl.when(i == 0)
    def _():
        acc[...] = jnp.zeros_like(acc)

    q = q_ref[0]
    used = cnt_ref[row] * tile
    rows = lax.broadcasted_iota(jnp.int32, q.shape, 0)
    q = jnp.where(rows < used, q, jnp.zeros_like(q))
    hidden = lax.dot_general(b_ref[0], q, (((0,), (0,)), ((), ())), preferred_element_type=F32)
    scaled = (hidden * d_ref[pl.ds(i, 1), :]).astype(BF16)
    y = lax.dot_general(scaled, q, (((1,), (1,)), ((), ())), preferred_element_type=F32)
    for k in range(kdom):
        part = y[:, k * tile : (k + 1) * tile].astype(BF16).astype(F32)
        s = slot_ref[dom_ref[row, k]]
        acc[:, s] += part.reshape(blocks, cols, tile)

    @pl.when(i == own - 1)
    def _():
        copies = []
        for j in range(blocks):
            stage[j] = acc[j].astype(BF16)
            copies.append(pltpu.make_async_copy(stage.at[j], out_ref.at[j], sems.at[j]))
            copies[-1].start()
        for copy in copies:
            copy.wait()


def reduce_kernel(g_ref, out_ref, own, rc, sa, sb, ra, rb, sa2, sb2, ra2, rb2, sz, zin, fs,
                  l_sem, cs, cr, as_, ar, bs, br, as2, ar2, bs2, br2, zs, zr):
    g = lax.axis_index("grp")
    o = lax.axis_index("occ")
    x, y = g % NX, g // NX
    core, z = o % NC, o // NC
    half = own.shape[-2] // 2
    lo, hi = pl.ds(0, half), pl.ds(half, half)
    to_core = {"grp": g, "occ": z * NC + 1 - core}
    to_x = {"grp": y * NX + 1 - x, "occ": o}
    to_y = {"grp": (1 - y) * NX + x, "occ": o}
    dest = [3 - 3 * (z // 2), (2 + 3 * z) % 5, 1 + z % 2, z]
    down = [z // 2, z % 2, z // 2]
    middle = z % 3

    barrier = pltpu.get_barrier_semaphore()
    for dev in (to_core, to_x, to_y):
        pl.semaphore_signal(barrier, inc=1, device_id=dev, device_id_type=MESH)

    @pl.when(z > 0)
    def _():
        pl.semaphore_signal(barrier, inc=1, device_id={"grp": g, "occ": o - NC}, device_id_type=MESH)

    @pl.when(z < NZ - 1)
    def _():
        pl.semaphore_signal(barrier, inc=1, device_id={"grp": g, "occ": o + NC}, device_id_type=MESH)

    loads = [pltpu.make_async_copy(g_ref.at[dest[t] * NC + core], own.at[t], l_sem.at[t]) for t in range(NZ)]
    for t in range(NZ):
        loads[t].start()
    pl.semaphore_wait(barrier, 4 + (middle + 1) // 2)

    def remote(src, dst, send, recv, dev):
        return pltpu.make_async_remote_copy(
            src_ref=src, dst_ref=dst, send_sem=send, recv_sem=recv, device_id=dev, device_id_type=MESH)

    c0 = [remote(g_ref.at[dest[t] * NC + 1 - core], rc.at[t], cs.at[t], cr.at[t], to_core) for t in range(NZ)]
    a1 = [remote(sa.at[t], ra.at[t], as_.at[t], ar.at[t], to_x) for t in range(NZ)]
    b1 = [remote(sb.at[t], rb.at[t], bs.at[t], br.at[t], to_y) for t in range(NZ)]
    a2 = [remote(sa2.at[t], ra2.at[t], as2.at[t], ar2.at[t], to_y) for t in range(NZ)]
    b2 = [remote(sb2.at[t], rb2.at[t], bs2.at[t], br2.at[t], to_x) for t in range(NZ)]
    zc = []
    for t in range(NZ - 1):
        to_z = {"grp": g, "occ": (z + 1 - 2 * down[t]) * NC + core}
        zc.append(remote(sz.at[t], zin.at[down[t], dest[t]], zs.at[t], zr.at[down[t], dest[t]], to_z))

    for t in range(NZ):
        c0[t].start()

    def both(t, iy, ix, rows):
        return own[t, iy, ix, :, rows, :].astype(F32) + rc[t, iy, ix, :, rows, :].astype(F32)

    def first(t):
        loads[t].wait()
        c0[t].wait_recv()
        for j in range(NY):
            sa[t, j] = both(t, j, 1 - x, lo).astype(BF16)
        a1[t].start()
        for j in range(NX):
            sb[t, j] = both(t, 1 - y, j, hi).astype(BF16)
        b1[t].start()

    def second(t):
        a1[t].wait_recv()
        sa2[t] = (both(t, 1 - y, x, lo) + ra[t, 1 - y].astype(F32)).astype(BF16)
        a2[t].start()
        b1[t].wait_recv()
        sb2[t] = (both(t, y, 1 - x, hi) + rb[t, 1 - x].astype(F32)).astype(BF16)
        b2[t].start()

    def plane(t):
        a2[t].wait_recv()
        fs[:, lo, :] = both(t, y, x, lo) + ra[t, y].astype(F32) + ra2[t].astype(F32)
        b2[t].wait_recv()
        fs[:, hi, :] = both(t, y, x, hi) + rb[t, x].astype(F32) + rb2[t].astype(F32)

    def edge(t):
        @pl.when(middle == 0)
        def _():
            plane(t)
            sz[t] = fs[...].astype(BF16)
            zc[t].start()

    def inner(t):
        @pl.when(middle != 0)
        def _():
            plane(t)
            zc[t].wait_recv()
            sz[t] = (fs[...] + zin[down[t], dest[t]].astype(F32)).astype(BF16)
            zc[t].start()

    first(0)
    first(1)
    second(0)
    first(2)
    second(1)
    edge(0)
    first(3)
    second(2)
    inner(0)
    edge(1)
    second(3)
    inner(1)
    edge(2)
    inner(2)
    plane(3)

    def landed(way):
        dev = {"grp": g, "occ": z * NC + 1 - core}
        remote(sz.at[0], zin.at[way, z], zs.at[0], zr.at[way, z], dev).wait_recv()
        fs[...] += zin[way, z].astype(F32)

    @pl.when(z > 0)
    def _():
        landed(0)

    @pl.when(z < NZ - 1)
    def _():
        landed(1)

    out_ref[...] = fs[...].astype(BF16)
    for t in range(NZ):
        for copy in (c0[t], a1[t], b1[t], a2[t], b2[t]):
            copy.wait_send()
    for t in range(NZ - 1):
        zc[t].wait_send()


def staged(b_ints, osv_vecs, inv_denom, domains, dom_count, owner_slot):
    own, rows, naux = b_ints.shape
    nosv = osv_vecs.shape[2]
    kdom = domains.shape[1]
    tile = rows // kdom
    ntiles = owner_slot.shape[0]
    blocks = NZ * NC
    cols = naux // blocks
    slots = ntiles // (NX * NY)
    partial_tiles = pl.pallas_call(
        functools.partial(tiles_kernel, kdom),
        out_shape=jax.ShapeDtypeStruct((blocks, ntiles, cols, tile), BF16),
        grid_spec=pltpu.PrefetchScalarGridSpec(
            num_scalar_prefetch=3,
            grid=(own,),
            in_specs=[
                pl.BlockSpec((1, rows, naux), lambda i, *_: (i, 0, 0)),
                pl.BlockSpec((1, rows, nosv), lambda i, *_: (i, 0, 0)),
                pl.BlockSpec((own, nosv), lambda i, *_: (0, 0)),
            ],
            out_specs=pl.BlockSpec(memory_space=pl.ANY),
            scratch_shapes=[
                pltpu.VMEM((blocks, ntiles, cols, tile), F32),
                pltpu.VMEM((blocks, ntiles, cols, tile), BF16),
                pltpu.SemaphoreType.DMA((blocks,)),
            ],
        ),
        compiler_params=pltpu.CompilerParams(vmem_limit_bytes=40 << 20),
        cost_estimate=pl.CostEstimate(
            flops=4 * own * rows * naux * nosv, bytes_accessed=11 << 20, transcendentals=0),
    )(domains, dom_count, owner_slot, b_ints, osv_vecs, inv_denom)
    partial_tiles = partial_tiles.reshape(blocks, NY, NX, slots, cols, tile)
    half = cols // 2
    vm = lambda *shape: pltpu.VMEM(shape, BF16)
    dma = lambda *shape: pltpu.SemaphoreType.DMA(shape)
    summed = pl.pallas_call(
        reduce_kernel,
        out_shape=jax.ShapeDtypeStruct((slots, cols, tile), BF16),
        in_specs=[pl.BlockSpec(memory_space=pl.ANY)],
        out_specs=pl.BlockSpec(memory_space=pltpu.VMEM),
        scratch_shapes=[
            vm(NZ, NY, NX, slots, cols, tile), vm(NZ, NY, NX, slots, cols, tile),
            vm(NZ, NY, slots, half, tile), vm(NZ, NX, slots, half, tile),
            vm(NZ, NY, slots, half, tile), vm(NZ, NX, slots, half, tile),
            vm(NZ, slots, half, tile), vm(NZ, slots, half, tile),
            vm(NZ, slots, half, tile), vm(NZ, slots, half, tile),
            vm(NZ - 1, slots, cols, tile), vm(2, NZ, slots, cols, tile),
            pltpu.VMEM((slots, cols, tile), F32),
        ] + [dma(NZ)] * 11 + [dma(NZ - 1), dma(2, NZ)],
        compiler_params=pltpu.CompilerParams(
            collective_id=0, has_side_effects=True, vmem_limit_bytes=40 << 20),
        cost_estimate=pl.CostEstimate(flops=4 << 20, bytes_accessed=7 << 20, transcendentals=0),
    )(partial_tiles)
    return jnp.swapaxes(summed, 0, 1)


def solution(mesh):
    fits = mesh.shape["grp"] == NX * NY and mesh.shape["occ"] == NZ * NC
    return jax.shard_map(
        staged if fits else general,
        mesh=mesh,
        in_specs=(
            P(("grp", "occ"), None, None),
            P(("grp", "occ"), None, None),
            P(("grp", "occ"), None),
            P("grp", None),
            P("grp"),
            P(),
        ),
        out_specs=P("occ", "grp", None),
        check_vma=False,
    )
```

```python
import jax
import jax.numpy as jnp
from jax import lax
from jax.experimental import pallas as pl
from jax.experimental.pallas import tpu as pltpu
from jax.sharding import PartitionSpec as P

MESH = pl.DeviceIdType.MESH
F32 = jnp.float32
BF16 = jnp.bfloat16
NX, NY, NZ, NC = 2, 2, 4, 2


def general(b_ints, osv_vecs, inv_denom, domains, dom_count, owner_slot):
    own = b_ints.shape[0]
    kdom = domains.shape[1]
    tile = b_ints.shape[1] // kdom
    ntiles = owner_slot.shape[0]
    tiles_ids = jnp.arange(ntiles, dtype=jnp.int32)
    keep_all = jnp.arange(kdom, dtype=jnp.int32)[None, :] < dom_count[:, None]
    looked = jnp.sum(jnp.where(domains[:, :, None] == tiles_ids, owner_slot, 0), axis=-1)
    slot_all = jnp.where(keep_all, looked, -1)
    start = lax.axis_index("occ") * own
    keep = lax.dynamic_slice_in_dim(keep_all, start, own, 0)
    rowmask = jnp.repeat(keep, tile, axis=1).astype(BF16)
    masked = b_ints * rowmask[:, :, None]
    hidden = jnp.einsum("ikn,ikp->inp", osv_vecs, masked, preferred_element_type=F32)
    scaled = (hidden * inv_denom[:, :, None]).astype(BF16)
    amp = jnp.einsum("ikn,inp->pik", osv_vecs, scaled, preferred_element_type=F32)
    amp = (amp * rowmask[None].astype(F32)).astype(BF16)
    got = lax.all_to_all(amp, "occ", split_axis=0, concat_axis=1, tiled=True)
    inst = got.reshape(got.shape[0], -1, tile)
    onehot = (slot_all.reshape(-1)[None, :] == tiles_ids[:, None]).astype(BF16)
    partial_sum = jnp.einsum("sn,pna->psa", onehot, inst, preferred_element_type=F32)
    summed = lax.psum_scatter(partial_sum, "grp", scatter_dimension=1, tiled=True)
    return summed.astype(BF16)


def fused_kernel(dom_ref, cnt_ref, slot_ref, d_ref, b_hbm, q_hbm, out_ref,
                 b_v, q_v, tiles, tab_v, tab_s, give, own, rc, sa, sb, ra, rb, sa2, sb2, ra2, rb2, sz, zin, fs,
                 t_sem, b_sem, q_sem, cs, cr, as_, ar, bs, br, as2, ar2, bs2, br2, zs, zr):
    g = lax.axis_index("grp")
    o = lax.axis_index("occ")
    x, y = g % NX, g // NX
    core, z = o % NC, o // NC
    norb, _, _ = b_v.shape
    kdom = dom_ref.shape[0]
    ntiles, cols, tile = own.shape[1:]
    blocks = tiles.shape[1]
    slots = ntiles // (NX * NY)
    half = cols // 2
    lo, hi = pl.ds(0, half), pl.ds(half, half)
    to_core = {"grp": g, "occ": z * NC + 1 - core}
    to_x = {"grp": y * NX + 1 - x, "occ": o}
    to_y = {"grp": (1 - y) * NX + x, "occ": o}
    dest = [3 - 3 * (z // 2), (2 + 3 * z) % 5, 1 + z % 2, z]
    down = [z // 2, z % 2, z // 2]
    middle = z % 3

    b_in = [pltpu.make_async_copy(b_hbm.at[i], b_v.at[i], b_sem.at[i]) for i in range(norb)]
    q_in = [pltpu.make_async_copy(q_hbm.at[i], q_v.at[i], q_sem.at[i]) for i in range(norb)]
    for i in range(norb):
        q_in[i].start()
        b_in[i].start()

    barrier = pltpu.get_barrier_semaphore()
    for dev in (to_core, to_x, to_y):
        pl.semaphore_signal(barrier, inc=1, device_id=dev, device_id_type=MESH)

    @pl.when(z > 0)
    def _():
        pl.semaphore_signal(barrier, inc=1, device_id={"grp": g, "occ": o - NC}, device_id_type=MESH)

    @pl.when(z < NZ - 1)
    def _():
        pl.semaphore_signal(barrier, inc=1, device_id={"grp": g, "occ": o + NC}, device_id_type=MESH)

    members = dom_ref.shape[1]
    mine = lax.broadcasted_iota(jnp.int32, (norb, members), 1) == (
        o * norb + lax.broadcasted_iota(jnp.int32, (norb, members), 0))

    def pick(row):
        return jnp.sum(jnp.where(mine, row, 0), axis=1, keepdims=True)

    count = pick(cnt_ref[...])
    wide = (norb, tab_v.shape[1])
    spot = lax.broadcasted_iota(jnp.int32, wide, 1)
    first_tile = lax.broadcasted_iota(jnp.int32, wide, 0) * kdom
    ids = lax.broadcasted_iota(jnp.int32, (norb, ntiles), 1)
    tab = jnp.full(wide, norb * kdom, jnp.int32)
    for k in range(kdom):
        chosen = pick(dom_ref[k : k + 1, :])
        slot = jnp.sum(jnp.where(ids == chosen, slot_ref[...], 0), axis=1, keepdims=True)
        tab = jnp.where((spot == slot) & (count > k), first_tile + k, tab)
    tab_v[...] = tab
    to_smem = pltpu.make_async_copy(tab_v, tab_s, t_sem)
    to_smem.start()
    tiles[norb * kdom] = jnp.zeros(tiles.shape[1:], BF16)

    for i in range(norb):
        q_in[i].wait()
        b_in[i].wait()
        q = q_v[i]
        rows = lax.broadcasted_iota(jnp.int32, q.shape, 0)
        q = jnp.where(rows < count[i : i + 1, :] * tile, q, jnp.zeros_like(q))
        hidden = lax.dot_general(b_v[i], q, (((0,), (0,)), ((), ())), preferred_element_type=F32)
        scaled = (hidden * d_ref[i : i + 1, :]).astype(BF16)
        amp = lax.dot_general(scaled, q, (((1,), (1,)), ((), ())), preferred_element_type=F32)
        for k in range(kdom):
            part = amp[:, k * tile : (k + 1) * tile].astype(BF16)
            tiles[i * kdom + k] = part.reshape(blocks, cols, tile)
    to_smem.wait()
    pl.semaphore_wait(barrier, 4 + (middle + 1) // 2)

    def remote(src, dst, send, recv, dev):
        return pltpu.make_async_remote_copy(
            src_ref=src, dst_ref=dst, send_sem=send, recv_sem=recv, device_id=dev, device_id_type=MESH)

    c0 = [remote(give.at[t], rc.at[t], cs.at[t], cr.at[t], to_core) for t in range(NZ)]
    a1 = [remote(sa.at[t], ra.at[t], as_.at[t], ar.at[t], to_x) for t in range(NZ)]
    b1 = [remote(sb.at[t], rb.at[t], bs.at[t], br.at[t], to_y) for t in range(NZ)]
    a2 = [remote(sa2.at[t], ra2.at[t], as2.at[t], ar2.at[t], to_y) for t in range(NZ)]
    b2 = [remote(sb2.at[t], rb2.at[t], bs2.at[t], br2.at[t], to_x) for t in range(NZ)]
    zc = []
    for t in range(NZ - 1):
        to_z = {"grp": g, "occ": (z + 1 - 2 * down[t]) * NC + core}
        zc.append(remote(sz.at[t], zin.at[down[t], dest[t]], zs.at[t], zr.at[down[t], dest[t]], to_z))

    def gather(block, into):
        @pl.loop(0, ntiles, unroll=4)
        def _(s):
            terms = [tiles[tab_s[i, s], block].astype(F32) for i in range(norb)]
            while len(terms) > 1:
                terms = [sum(terms[j : j + 2][1:], terms[j]) for j in range(0, len(terms), 2)]
            into[s] = terms[0].astype(BF16)

    def partner(t):
        gather(dest[t] * NC + 1 - core, give.at[t])
        c0[t].start()

    def keep(t):
        gather(dest[t] * NC + core, own.at[t])

    def both(t, iy, ix, rows):
        at = pl.ds((iy * NX + ix) * slots, slots)
        return own[t, at, rows, :].astype(F32) + rc[t, at, rows, :].astype(F32)

    def first(t):
        c0[t].wait_recv()
        for j in range(NY):
            sa[t, j] = both(t, j, 1 - x, lo).astype(BF16)
        a1[t].start()
        for j in range(NX):
            sb[t, j] = both(t, 1 - y, j, hi).astype(BF16)
        b1[t].start()

    def second(t):
        a1[t].wait_recv()
        sa2[t] = (both(t, 1 - y, x, lo) + ra[t, 1 - y].astype(F32)).astype(BF16)
        a2[t].start()
        b1[t].wait_recv()
        sb2[t] = (both(t, y, 1 - x, hi) + rb[t, 1 - x].astype(F32)).astype(BF16)
        b2[t].start()

    def plane(t):
        a2[t].wait_recv()
        fs[:, lo, :] = both(t, y, x, lo) + ra[t, y].astype(F32) + ra2[t].astype(F32)
        b2[t].wait_recv()
        fs[:, hi, :] = both(t, y, x, hi) + rb[t, x].astype(F32) + rb2[t].astype(F32)

    def edge(t):
        @pl.when(middle == 0)
        def _():
            plane(t)
            sz[t] = fs[...].astype(BF16)
            zc[t].start()

    def inner(t):
        @pl.when(middle != 0)
        def _():
            plane(t)
            zc[t].wait_recv()
            sz[t] = (fs[...] + zin[down[t], dest[t]].astype(F32)).astype(BF16)
            zc[t].start()

    partner(0)
    keep(0)
    first(0)
    partner(1)
    keep(1)
    first(1)
    second(0)
    partner(2)
    keep(2)
    first(2)
    second(1)
    edge(0)
    partner(3)
    keep(3)
    first(3)
    second(2)
    inner(0)
    edge(1)
    second(3)
    inner(1)
    edge(2)
    inner(2)
    plane(3)

    def landed(way):
        remote(sz.at[0], zin.at[way, z], zs.at[0], zr.at[way, z], to_core).wait_recv()
        fs[...] += zin[way, z].astype(F32)

    @pl.when(z > 0)
    def _():
        landed(0)

    @pl.when(z < NZ - 1)
    def _():
        landed(1)

    out_ref[...] = fs[...].astype(BF16)
    for t in range(NZ):
        for copy in (c0[t], a1[t], b1[t], a2[t], b2[t]):
            copy.wait_send()
    for t in range(NZ - 1):
        zc[t].wait_send()


def staged(b_ints, osv_vecs, inv_denom, domains, dom_count, owner_slot):
    norb, rows, naux = b_ints.shape
    nosv = osv_vecs.shape[2]
    members, kdom = domains.shape
    tile = rows // kdom
    ntiles = owner_slot.shape[0]
    blocks = NZ * NC
    cols = naux // blocks
    slots = ntiles // (NX * NY)
    half = cols // 2
    lanes = -(-ntiles // 128) * 128
    vm = lambda *shape: pltpu.VMEM(shape, BF16)
    dma = lambda *shape: pltpu.SemaphoreType.DMA(shape)
    in_vmem = pl.BlockSpec(memory_space=pltpu.VMEM)
    summed = pl.pallas_call(
        fused_kernel,
        out_shape=jax.ShapeDtypeStruct((slots, cols, tile), BF16),
        in_specs=[in_vmem] * 4 + [pl.BlockSpec(memory_space=pl.ANY)] * 2,
        out_specs=in_vmem,
        scratch_shapes=[
            vm(norb, rows, naux), vm(norb, rows, nosv), vm(norb * kdom + 1, blocks, cols, tile),
            pltpu.VMEM((norb, lanes), jnp.int32), pltpu.SMEM((norb, lanes), jnp.int32),
            vm(NZ, ntiles, cols, tile), vm(NZ, ntiles, cols, tile), vm(NZ, ntiles, cols, tile),
            vm(NZ, NY, slots, half, tile), vm(NZ, NX, slots, half, tile),
            vm(NZ, NY, slots, half, tile), vm(NZ, NX, slots, half, tile),
            vm(NZ, slots, half, tile), vm(NZ, slots, half, tile),
            vm(NZ, slots, half, tile), vm(NZ, slots, half, tile),
            vm(NZ - 1, slots, cols, tile), vm(2, NZ, slots, cols, tile),
            pltpu.VMEM((slots, cols, tile), F32),
            pltpu.SemaphoreType.DMA, dma(norb), dma(norb),
        ] + [dma(NZ)] * 10 + [dma(NZ - 1), dma(2, NZ)],
        compiler_params=pltpu.CompilerParams(
            collective_id=0, has_side_effects=True, vmem_limit_bytes=56 << 20),
        cost_estimate=pl.CostEstimate(
            flops=4 * norb * rows * naux * nosv, bytes_accessed=5 << 20, transcendentals=0),
    )(domains.T, dom_count.reshape(1, members), owner_slot.reshape(1, ntiles), inv_denom, b_ints, osv_vecs)
    return jnp.swapaxes(summed, 0, 1)


def solution(mesh):
    fits = mesh.shape["grp"] == NX * NY and mesh.shape["occ"] == NZ * NC
    return jax.shard_map(
        staged if fits else general,
        mesh=mesh,
        in_specs=(
            P(("grp", "occ"), None, None),
            P(("grp", "occ"), None, None),
            P(("grp", "occ"), None),
            P("grp", None),
            P("grp"),
            P(),
        ),
        out_specs=P("occ", "grp", None),
        check_vma=False,
    )
```

```python
import jax
import jax.numpy as jnp
from jax import lax
from jax.experimental import pallas as pl
from jax.experimental.pallas import tpu as pltpu
from jax.sharding import PartitionSpec as P

MESH = pl.DeviceIdType.MESH
F32 = jnp.float32
BF16 = jnp.bfloat16
NX, NY, NZ, NC = 2, 2, 4, 2
PARTS = 2
NU = NZ * PARTS


def general(b_ints, osv_vecs, inv_denom, domains, dom_count, owner_slot):
    own = b_ints.shape[0]
    kdom = domains.shape[1]
    tile = b_ints.shape[1] // kdom
    ntiles = owner_slot.shape[0]
    tiles_ids = jnp.arange(ntiles, dtype=jnp.int32)
    keep_all = jnp.arange(kdom, dtype=jnp.int32)[None, :] < dom_count[:, None]
    looked = jnp.sum(jnp.where(domains[:, :, None] == tiles_ids, owner_slot, 0), axis=-1)
    slot_all = jnp.where(keep_all, looked, -1)
    start = lax.axis_index("occ") * own
    keep = lax.dynamic_slice_in_dim(keep_all, start, own, 0)
    rowmask = jnp.repeat(keep, tile, axis=1).astype(BF16)
    masked = b_ints * rowmask[:, :, None]
    hidden = jnp.einsum("ikn,ikp->inp", osv_vecs, masked, preferred_element_type=F32)
    scaled = (hidden * inv_denom[:, :, None]).astype(BF16)
    amp = jnp.einsum("ikn,inp->pik", osv_vecs, scaled, preferred_element_type=F32)
    amp = (amp * rowmask[None].astype(F32)).astype(BF16)
    got = lax.all_to_all(amp, "occ", split_axis=0, concat_axis=1, tiled=True)
    inst = got.reshape(got.shape[0], -1, tile)
    onehot = (slot_all.reshape(-1)[None, :] == tiles_ids[:, None]).astype(BF16)
    partial_sum = jnp.einsum("sn,pna->psa", onehot, inst, preferred_element_type=F32)
    summed = lax.psum_scatter(partial_sum, "grp", scatter_dimension=1, tiled=True)
    return summed.astype(BF16)


def fused_kernel(dom_ref, cnt_ref, slot_ref, d_ref, b_hbm, q_hbm, out_ref,
                 b_v, q_v, tiles, tab_v, tab_s, give, own, rc, sa, sb, ra, rb, sa2, sb2, ra2, rb2, sz, zin, fs,
                 t_sem, b_sem, q_sem, cs, cr, as_, ar, bs, br, as2, ar2, bs2, br2, zs, zr):
    g = lax.axis_index("grp")
    o = lax.axis_index("occ")
    x, y = g % NX, g // NX
    core, z = o % NC, o // NC
    norb, _, _ = b_v.shape
    kdom = dom_ref.shape[0]
    ntiles = slot_ref.shape[1]
    cols, tile = own.shape[2:]
    blocks = tiles.shape[1]
    part_slots = own.shape[1] // (NX * NY)
    slots = part_slots * PARTS
    half = cols // 2
    lo, hi = pl.ds(0, half), pl.ds(half, half)
    to_core = {"grp": g, "occ": z * NC + 1 - core}
    to_x = {"grp": y * NX + 1 - x, "occ": o}
    to_y = {"grp": (1 - y) * NX + x, "occ": o}
    dest = [d for d in (3 - 3 * (z // 2), (2 + 3 * z) % 5, 1 + z % 2, z) for _ in range(PARTS)]
    down = [d for d in (z // 2, z % 2, z // 2) for _ in range(PARTS)]
    late = NU - PARTS
    middle = z % 3

    b_in = [pltpu.make_async_copy(b_hbm.at[i], b_v.at[i], b_sem.at[i]) for i in range(norb)]
    q_in = [pltpu.make_async_copy(q_hbm.at[i], q_v.at[i], q_sem.at[i]) for i in range(norb)]
    for i in range(norb):
        q_in[i].start()
        b_in[i].start()

    barrier = pltpu.get_barrier_semaphore()
    for dev in (to_core, to_x, to_y):
        pl.semaphore_signal(barrier, inc=1, device_id=dev, device_id_type=MESH)

    @pl.when(z > 0)
    def _():
        pl.semaphore_signal(barrier, inc=1, device_id={"grp": g, "occ": o - NC}, device_id_type=MESH)

    @pl.when(z < NZ - 1)
    def _():
        pl.semaphore_signal(barrier, inc=1, device_id={"grp": g, "occ": o + NC}, device_id_type=MESH)

    members = dom_ref.shape[1]
    mine = lax.broadcasted_iota(jnp.int32, (norb, members), 1) == (
        o * norb + lax.broadcasted_iota(jnp.int32, (norb, members), 0))

    def pick(row):
        return jnp.sum(jnp.where(mine, row, 0), axis=1, keepdims=True)

    count = pick(cnt_ref[...])
    wide = (norb, tab_v.shape[1])
    spot = lax.broadcasted_iota(jnp.int32, wide, 1)
    first_tile = lax.broadcasted_iota(jnp.int32, wide, 0) * kdom
    ids = lax.broadcasted_iota(jnp.int32, (norb, ntiles), 1)
    tab = jnp.full(wide, norb * kdom, jnp.int32)
    for k in range(kdom):
        chosen = pick(dom_ref[k : k + 1, :])
        slot = jnp.sum(jnp.where(ids == chosen, slot_ref[...], 0), axis=1, keepdims=True)
        tab = jnp.where((spot == slot) & (count > k), first_tile + k, tab)
    tab_v[...] = tab
    to_smem = pltpu.make_async_copy(tab_v, tab_s, t_sem)
    to_smem.start()
    tiles[norb * kdom] = jnp.zeros(tiles.shape[1:], BF16)

    for i in range(norb):
        q_in[i].wait()
        b_in[i].wait()
        q = q_v[i]
        rows = lax.broadcasted_iota(jnp.int32, q.shape, 0)
        q = jnp.where(rows < count[i : i + 1, :] * tile, q, jnp.zeros_like(q))
        hidden = lax.dot_general(b_v[i], q, (((0,), (0,)), ((), ())), preferred_element_type=F32)
        scaled = (hidden * d_ref[i : i + 1, :]).astype(BF16)
        amp = lax.dot_general(scaled, q, (((1,), (1,)), ((), ())), preferred_element_type=F32)
        for k in range(kdom):
            part = amp[:, k * tile : (k + 1) * tile].astype(BF16)
            tiles[i * kdom + k] = part.reshape(blocks, cols, tile)
    to_smem.wait()
    pl.semaphore_wait(barrier, 4 + (middle + 1) // 2)

    def remote(src, dst, send, recv, dev):
        return pltpu.make_async_remote_copy(
            src_ref=src, dst_ref=dst, send_sem=send, recv_sem=recv, device_id=dev, device_id_type=MESH)

    c0 = [remote(give.at[t], rc.at[t], cs.at[t], cr.at[t], to_core) for t in range(NU)]
    a1 = [remote(sa.at[t], ra.at[t], as_.at[t], ar.at[t], to_x) for t in range(NU)]
    b1 = [remote(sb.at[t], rb.at[t], bs.at[t], br.at[t], to_y) for t in range(NU)]
    a2 = [remote(sa2.at[t], ra2.at[t], as2.at[t], ar2.at[t], to_y) for t in range(NU)]
    b2 = [remote(sb2.at[t], rb2.at[t], bs2.at[t], br2.at[t], to_x) for t in range(NU)]
    zc = []
    for t in range(late):
        to_z = {"grp": g, "occ": (z + 1 - 2 * down[t]) * NC + core}
        lands = dest[t] * PARTS + t % PARTS
        zc.append(remote(sz.at[t], zin.at[down[t], lands], zs.at[t], zr.at[down[t], lands], to_z))

    def gather(t, block, into):
        for q in range(NX * NY):
            @pl.loop(0, part_slots, unroll=4)
            def _(j):
                s = q * slots + (t % PARTS) * part_slots + j
                terms = [tiles[tab_s[i, s], block].astype(F32) for i in range(norb)]
                while len(terms) > 1:
                    terms = [sum(terms[n : n + 2][1:], terms[n]) for n in range(0, len(terms), 2)]
                into[q * part_slots + j] = terms[0].astype(BF16)

    def partner(t):
        gather(t, dest[t] * NC + 1 - core, give.at[t])
        c0[t].start()

    def keep(t):
        gather(t, dest[t] * NC + core, own.at[t])

    def both(t, iy, ix, rows):
        at = pl.ds((iy * NX + ix) * part_slots, part_slots)
        return own[t, at, rows, :].astype(F32) + rc[t, at, rows, :].astype(F32)

    def first(t):
        c0[t].wait_recv()
        for j in range(NY):
            sa[t, j] = both(t, j, 1 - x, lo).astype(BF16)
        a1[t].start()
        for j in range(NX):
            sb[t, j] = both(t, 1 - y, j, hi).astype(BF16)
        b1[t].start()

    def second(t):
        a1[t].wait_recv()
        sa2[t] = (both(t, 1 - y, x, lo) + ra[t, 1 - y].astype(F32)).astype(BF16)
        a2[t].start()
        b1[t].wait_recv()
        sb2[t] = (both(t, y, 1 - x, hi) + rb[t, 1 - x].astype(F32)).astype(BF16)
        b2[t].start()

    def plane(t):
        a2[t].wait_recv()
        fs[:, lo, :] = both(t, y, x, lo) + ra[t, y].astype(F32) + ra2[t].astype(F32)
        b2[t].wait_recv()
        fs[:, hi, :] = both(t, y, x, hi) + rb[t, x].astype(F32) + rb2[t].astype(F32)

    def edge(t):
        @pl.when(middle == 0)
        def _():
            plane(t)
            sz[t] = fs[...].astype(BF16)
            zc[t].start()

    def inner(t):
        @pl.when(middle != 0)
        def _():
            plane(t)
            zc[t].wait_recv()
            sz[t] = (fs[...] + zin[down[t], dest[t] * PARTS + t % PARTS].astype(F32)).astype(BF16)
            zc[t].start()

    def landed(t, way):
        at = z * PARTS + t % PARTS
        remote(sz.at[0], zin.at[way, at], zs.at[0], zr.at[way, at], to_core).wait_recv()
        fs[...] += zin[way, at].astype(F32)

    def final(t):
        plane(t)

        @pl.when(z > 0)
        def _():
            landed(t, 0)

        @pl.when(z < NZ - 1)
        def _():
            landed(t, 1)

        out_ref[pl.ds((t % PARTS) * part_slots, part_slots)] = fs[...].astype(BF16)

    for step in range(NU + 1):
        if step < NU:
            partner(step)
            keep(step)
            first(step)
        if step >= 1:
            second(step - 1)
        if 0 <= step - 2 < late:
            edge(step - 2)
        if 0 <= step - 3 < late:
            inner(step - 3)
    for t in range(late, NU):
        final(t)

    for t in range(NU):
        for copy in (c0[t], a1[t], b1[t], a2[t], b2[t]):
            copy.wait_send()
    for t in range(late):
        zc[t].wait_send()


def staged(b_ints, osv_vecs, inv_denom, domains, dom_count, owner_slot):
    norb, rows, naux = b_ints.shape
    nosv = osv_vecs.shape[2]
    members, kdom = domains.shape
    tile = rows // kdom
    ntiles = owner_slot.shape[0]
    blocks = NZ * NC
    cols = naux // blocks
    slots = ntiles // (NX * NY)
    half = cols // 2
    part = slots // PARTS
    quarter = ntiles // PARTS
    lanes = -(-ntiles // 128) * 128
    vm = lambda *shape: pltpu.VMEM(shape, BF16)
    dma = lambda *shape: pltpu.SemaphoreType.DMA(shape)
    in_vmem = pl.BlockSpec(memory_space=pltpu.VMEM)
    summed = pl.pallas_call(
        fused_kernel,
        out_shape=jax.ShapeDtypeStruct((slots, cols, tile), BF16),
        in_specs=[in_vmem] * 4 + [pl.BlockSpec(memory_space=pltpu.HBM)] * 2,
        out_specs=in_vmem,
        scratch_shapes=[
            vm(norb, rows, naux), vm(norb, rows, nosv), vm(norb * kdom + 1, blocks, cols, tile),
            pltpu.VMEM((norb, lanes), jnp.int32), pltpu.SMEM((norb, lanes), jnp.int32),
            vm(NU, quarter, cols, tile), vm(NU, quarter, cols, tile), vm(NU, quarter, cols, tile),
            vm(NU, NY, part, half, tile), vm(NU, NX, part, half, tile),
            vm(NU, NY, part, half, tile), vm(NU, NX, part, half, tile),
            vm(NU, part, half, tile), vm(NU, part, half, tile),
            vm(NU, part, half, tile), vm(NU, part, half, tile),
            vm(NU - PARTS, part, cols, tile), vm(2, NU, part, cols, tile),
            pltpu.VMEM((part, cols, tile), F32),
            pltpu.SemaphoreType.DMA, dma(norb), dma(norb),
        ] + [dma(NU)] * 10 + [dma(NU - PARTS), dma(2, NU)],
        compiler_params=pltpu.CompilerParams(
            collective_id=0, has_side_effects=True, vmem_limit_bytes=56 << 20),
        cost_estimate=pl.CostEstimate(
            flops=4 * norb * rows * naux * nosv, bytes_accessed=5 << 20, transcendentals=0),
    )(domains.T, dom_count.reshape(1, members), owner_slot.reshape(1, ntiles), inv_denom, b_ints, osv_vecs)
    return jnp.swapaxes(summed, 0, 1)


def solution(mesh):
    fits = mesh.shape["grp"] == NX * NY and mesh.shape["occ"] == NZ * NC
    return jax.shard_map(
        staged if fits else general,
        mesh=mesh,
        in_specs=(
            P(("grp", "occ"), None, None),
            P(("grp", "occ"), None, None),
            P(("grp", "occ"), None),
            P("grp", None),
            P("grp"),
            P(),
        ),
        out_specs=P("occ", "grp", None),
        check_vma=False,
    )
```

```python
import jax
import jax.numpy as jnp
from jax import lax
from jax.experimental import pallas as pl
from jax.experimental.pallas import tpu as pltpu
from jax.sharding import PartitionSpec as P

MESH = pl.DeviceIdType.MESH
F32 = jnp.float32
BF16 = jnp.bfloat16
NX, NY, NZ, NC = 2, 2, 4, 2


def general(b_ints, osv_vecs, inv_denom, domains, dom_count, owner_slot):
    own = b_ints.shape[0]
    kdom = domains.shape[1]
    tile = b_ints.shape[1] // kdom
    ntiles = owner_slot.shape[0]
    tiles_ids = jnp.arange(ntiles, dtype=jnp.int32)
    keep_all = jnp.arange(kdom, dtype=jnp.int32)[None, :] < dom_count[:, None]
    looked = jnp.sum(jnp.where(domains[:, :, None] == tiles_ids, owner_slot, 0), axis=-1)
    slot_all = jnp.where(keep_all, looked, -1)
    start = lax.axis_index("occ") * own
    keep = lax.dynamic_slice_in_dim(keep_all, start, own, 0)
    rowmask = jnp.repeat(keep, tile, axis=1).astype(BF16)
    masked = b_ints * rowmask[:, :, None]
    hidden = jnp.einsum("ikn,ikp->inp", osv_vecs, masked, preferred_element_type=F32)
    scaled = (hidden * inv_denom[:, :, None]).astype(BF16)
    amp = jnp.einsum("ikn,inp->pik", osv_vecs, scaled, preferred_element_type=F32)
    amp = (amp * rowmask[None].astype(F32)).astype(BF16)
    got = lax.all_to_all(amp, "occ", split_axis=0, concat_axis=1, tiled=True)
    inst = got.reshape(got.shape[0], -1, tile)
    onehot = (slot_all.reshape(-1)[None, :] == tiles_ids[:, None]).astype(BF16)
    partial_sum = jnp.einsum("sn,pna->psa", onehot, inst, preferred_element_type=F32)
    summed = lax.psum_scatter(partial_sum, "grp", scatter_dimension=1, tiled=True)
    return summed.astype(BF16)


def fused_kernel(dom_ref, cnt_ref, slot_ref, d_ref, b_hbm, q_hbm, out_ref,
                 b_v, q_v, tiles, tab_v, tab_s, give, own, rc, sa, sb, ra, rb, sa2, sb2, ra2, rb2, sz, zin, fs, turned,
                 t_sem, b_sem, q_sem, cs, cr, as_, ar, bs, br, as2, ar2, bs2, br2, zs, zr):
    g = lax.axis_index("grp")
    o = lax.axis_index("occ")
    x, y = g % NX, g // NX
    core, z = o % NC, o // NC
    norb, _, _ = b_v.shape
    kdom = dom_ref.shape[0]
    ntiles, cols, tile = own.shape[1:]
    blocks = tiles.shape[1]
    slots = ntiles // (NX * NY)
    half = cols // 2
    lo, hi = pl.ds(0, half), pl.ds(half, half)
    to_core = {"grp": g, "occ": z * NC + 1 - core}
    to_x = {"grp": y * NX + 1 - x, "occ": o}
    to_y = {"grp": (1 - y) * NX + x, "occ": o}
    dest = [3 - 3 * (z // 2), (2 + 3 * z) % 5, 1 + z % 2, z]
    down = [z // 2, z % 2, z // 2]
    middle = z % 3

    b_in = [pltpu.make_async_copy(b_hbm.at[i], b_v.at[i], b_sem.at[i]) for i in range(norb)]
    q_in = [pltpu.make_async_copy(q_hbm.at[i], q_v.at[i], q_sem.at[i]) for i in range(norb)]
    for i in range(norb):
        q_in[i].start()
        b_in[i].start()

    barrier = pltpu.get_barrier_semaphore()
    for dev in (to_core, to_x, to_y):
        pl.semaphore_signal(barrier, inc=1, device_id=dev, device_id_type=MESH)

    @pl.when(z > 0)
    def _():
        pl.semaphore_signal(barrier, inc=1, device_id={"grp": g, "occ": o - NC}, device_id_type=MESH)

    @pl.when(z < NZ - 1)
    def _():
        pl.semaphore_signal(barrier, inc=1, device_id={"grp": g, "occ": o + NC}, device_id_type=MESH)

    members = dom_ref.shape[1]
    mine = lax.broadcasted_iota(jnp.int32, (norb, members), 1) == (
        o * norb + lax.broadcasted_iota(jnp.int32, (norb, members), 0))

    def pick(row):
        return jnp.sum(jnp.where(mine, row, 0), axis=1, keepdims=True)

    count = pick(cnt_ref[...])
    wide = (norb, tab_v.shape[1])
    spot = lax.broadcasted_iota(jnp.int32, wide, 1)
    first_tile = lax.broadcasted_iota(jnp.int32, wide, 0) * kdom
    ids = lax.broadcasted_iota(jnp.int32, (norb, ntiles), 1)
    tab = jnp.full(wide, norb * kdom, jnp.int32)
    for k in range(kdom):
        chosen = pick(dom_ref[k : k + 1, :])
        slot = jnp.sum(jnp.where(ids == chosen, slot_ref[...], 0), axis=1, keepdims=True)
        tab = jnp.where((spot == slot) & (count > k), first_tile + k, tab)
    tab_v[...] = tab
    to_smem = pltpu.make_async_copy(tab_v, tab_s, t_sem)
    to_smem.start()
    tiles[norb * kdom] = jnp.zeros(tiles.shape[1:], BF16)

    for i in range(norb):
        q_in[i].wait()
        b_in[i].wait()
        q = q_v[i]
        rows = lax.broadcasted_iota(jnp.int32, q.shape, 0)
        q = jnp.where(rows < count[i : i + 1, :] * tile, q, jnp.zeros_like(q))
        hidden = lax.dot_general(b_v[i], q, (((0,), (0,)), ((), ())), preferred_element_type=F32)
        scaled = (hidden * d_ref[i : i + 1, :]).astype(BF16)
        amp = lax.dot_general(scaled, q, (((1,), (1,)), ((), ())), preferred_element_type=F32)
        for k in range(kdom):
            part = amp[:, k * tile : (k + 1) * tile].astype(BF16)
            tiles[i * kdom + k] = part.reshape(blocks, cols, tile)
    to_smem.wait()
    pl.semaphore_wait(barrier, 4 + (middle + 1) // 2)

    def remote(src, dst, send, recv, dev):
        return pltpu.make_async_remote_copy(
            src_ref=src, dst_ref=dst, send_sem=send, recv_sem=recv, device_id=dev, device_id_type=MESH)

    c0 = [remote(give.at[t], rc.at[t], cs.at[t], cr.at[t], to_core) for t in range(NZ)]
    a1 = [remote(sa.at[t], ra.at[t], as_.at[t], ar.at[t], to_x) for t in range(NZ)]
    b1 = [remote(sb.at[t], rb.at[t], bs.at[t], br.at[t], to_y) for t in range(NZ)]
    a2 = [remote(sa2.at[t], ra2.at[t], as2.at[t], ar2.at[t], to_y) for t in range(NZ)]
    b2 = [remote(sb2.at[t], rb2.at[t], bs2.at[t], br2.at[t], to_x) for t in range(NZ)]
    zc = []
    for t in range(NZ - 1):
        to_z = {"grp": g, "occ": (z + 1 - 2 * down[t]) * NC + core}
        zc.append(remote(sz.at[t], zin.at[down[t], dest[t]], zs.at[t], zr.at[down[t], dest[t]], to_z))

    def gather(block, into):
        @pl.loop(0, ntiles, unroll=4)
        def _(s):
            terms = [tiles[tab_s[i, s], block].astype(F32) for i in range(norb)]
            while len(terms) > 1:
                terms = [sum(terms[j : j + 2][1:], terms[j]) for j in range(0, len(terms), 2)]
            into[s] = terms[0].astype(BF16)

    def partner(t):
        gather(dest[t] * NC + 1 - core, give.at[t])
        c0[t].start()

    def keep(t):
        gather(dest[t] * NC + core, own.at[t])

    def both(t, iy, ix, rows):
        at = pl.ds((iy * NX + ix) * slots, slots)
        return own[t, at, rows, :].astype(F32) + rc[t, at, rows, :].astype(F32)

    def first(t):
        c0[t].wait_recv()
        for j in range(NY):
            sa[t, j] = both(t, j, 1 - x, lo).astype(BF16)
        a1[t].start()
        for j in range(NX):
            sb[t, j] = both(t, 1 - y, j, hi).astype(BF16)
        b1[t].start()

    def second(t):
        a1[t].wait_recv()
        sa2[t] = (both(t, 1 - y, x, lo) + ra[t, 1 - y].astype(F32)).astype(BF16)
        a2[t].start()
        b1[t].wait_recv()
        sb2[t] = (both(t, y, 1 - x, hi) + rb[t, 1 - x].astype(F32)).astype(BF16)
        b2[t].start()

    def plane(t):
        a2[t].wait_recv()
        fs[:, lo, :] = both(t, y, x, lo) + ra[t, y].astype(F32) + ra2[t].astype(F32)
        b2[t].wait_recv()
        fs[:, hi, :] = both(t, y, x, hi) + rb[t, x].astype(F32) + rb2[t].astype(F32)

    def edge(t):
        @pl.when(middle == 0)
        def _():
            plane(t)
            sz[t] = fs[...].astype(BF16)
            zc[t].start()

    def inner(t):
        @pl.when(middle != 0)
        def _():
            plane(t)
            zc[t].wait_recv()
            sz[t] = (fs[...] + zin[down[t], dest[t]].astype(F32)).astype(BF16)
            zc[t].start()

    partner(0)
    keep(0)
    first(0)
    partner(1)
    keep(1)
    first(1)
    second(0)
    partner(2)
    keep(2)
    first(2)
    second(1)
    edge(0)
    partner(3)
    keep(3)
    first(3)
    second(2)
    inner(0)
    edge(1)
    second(3)
    inner(1)
    edge(2)
    inner(2)
    plane(3)

    def landed(way):
        remote(sz.at[0], zin.at[way, z], zs.at[0], zr.at[way, z], to_core).wait_recv()
        fs[...] += zin[way, z].astype(F32)

    @pl.when(z > 0)
    def _():
        landed(0)

    @pl.when(z < NZ - 1)
    def _():
        landed(1)

    for s in range(slots):
        turned[:, s, :] = fs[s]
    out_ref[...] = turned[...].astype(BF16)
    for t in range(NZ):
        for copy in (c0[t], a1[t], b1[t], a2[t], b2[t]):
            copy.wait_send()
    for t in range(NZ - 1):
        zc[t].wait_send()


def staged(b_ints, osv_vecs, inv_denom, domains, dom_count, owner_slot):
    norb, rows, naux = b_ints.shape
    nosv = osv_vecs.shape[2]
    members, kdom = domains.shape
    tile = rows // kdom
    ntiles = owner_slot.shape[0]
    blocks = NZ * NC
    cols = naux // blocks
    slots = ntiles // (NX * NY)
    half = cols // 2
    lanes = -(-ntiles // 128) * 128
    vm = lambda *shape: pltpu.VMEM(shape, BF16)
    dma = lambda *shape: pltpu.SemaphoreType.DMA(shape)
    in_vmem = pl.BlockSpec(memory_space=pltpu.VMEM)
    return pl.pallas_call(
        fused_kernel,
        out_shape=jax.ShapeDtypeStruct((cols, slots, tile), BF16),
        in_specs=[in_vmem] * 4 + [pl.BlockSpec(memory_space=pl.ANY)] * 2,
        out_specs=in_vmem,
        scratch_shapes=[
            vm(norb, rows, naux), vm(norb, rows, nosv), vm(norb * kdom + 1, blocks, cols, tile),
            pltpu.VMEM((norb, lanes), jnp.int32), pltpu.SMEM((norb, lanes), jnp.int32),
            vm(NZ, ntiles, cols, tile), vm(NZ, ntiles, cols, tile), vm(NZ, ntiles, cols, tile),
            vm(NZ, NY, slots, half, tile), vm(NZ, NX, slots, half, tile),
            vm(NZ, NY, slots, half, tile), vm(NZ, NX, slots, half, tile),
            vm(NZ, slots, half, tile), vm(NZ, slots, half, tile),
            vm(NZ, slots, half, tile), vm(NZ, slots, half, tile),
            vm(NZ - 1, slots, cols, tile), vm(2, NZ, slots, cols, tile),
            pltpu.VMEM((slots, cols, tile), F32), pltpu.VMEM((cols, slots, tile), F32),
            pltpu.SemaphoreType.DMA, dma(norb), dma(norb),
        ] + [dma(NZ)] * 10 + [dma(NZ - 1), dma(2, NZ)],
        compiler_params=pltpu.CompilerParams(
            collective_id=0, has_side_effects=True, vmem_limit_bytes=56 << 20),
        cost_estimate=pl.CostEstimate(
            flops=4 * norb * rows * naux * nosv, bytes_accessed=5 << 20, transcendentals=0),
    )(domains.T, dom_count.reshape(1, members), owner_slot.reshape(1, ntiles), inv_denom, b_ints, osv_vecs)


def solution(mesh):
    fits = mesh.shape["grp"] == NX * NY and mesh.shape["occ"] == NZ * NC
    return jax.shard_map(
        staged if fits else general,
        mesh=mesh,
        in_specs=(
            P(("grp", "occ"), None, None),
            P(("grp", "occ"), None, None),
            P(("grp", "occ"), None),
            P("grp", None),
            P("grp"),
            P(),
        ),
        out_specs=P("occ", "grp", None),
        check_vma=False,
    )
```

```python
import jax
import jax.numpy as jnp
from jax import lax
from jax.experimental import pallas as pl
from jax.experimental.pallas import tpu as pltpu
from jax.sharding import PartitionSpec as P

MESH = pl.DeviceIdType.MESH
F32 = jnp.float32
BF16 = jnp.bfloat16
NX, NY, NZ, NC = 2, 2, 4, 2
PARTS = 2
NU = NZ * PARTS


def general(b_ints, osv_vecs, inv_denom, domains, dom_count, owner_slot):
    own = b_ints.shape[0]
    kdom = domains.shape[1]
    tile = b_ints.shape[1] // kdom
    ntiles = owner_slot.shape[0]
    tiles_ids = jnp.arange(ntiles, dtype=jnp.int32)
    keep_all = jnp.arange(kdom, dtype=jnp.int32)[None, :] < dom_count[:, None]
    looked = jnp.sum(jnp.where(domains[:, :, None] == tiles_ids, owner_slot, 0), axis=-1)
    slot_all = jnp.where(keep_all, looked, -1)
    start = lax.axis_index("occ") * own
    keep = lax.dynamic_slice_in_dim(keep_all, start, own, 0)
    rowmask = jnp.repeat(keep, tile, axis=1).astype(BF16)
    masked = b_ints * rowmask[:, :, None]
    hidden = jnp.einsum("ikn,ikp->inp", osv_vecs, masked, preferred_element_type=F32)
    scaled = (hidden * inv_denom[:, :, None]).astype(BF16)
    amp = jnp.einsum("ikn,inp->pik", osv_vecs, scaled, preferred_element_type=F32)
    amp = (amp * rowmask[None].astype(F32)).astype(BF16)
    got = lax.all_to_all(amp, "occ", split_axis=0, concat_axis=1, tiled=True)
    inst = got.reshape(got.shape[0], -1, tile)
    onehot = (slot_all.reshape(-1)[None, :] == tiles_ids[:, None]).astype(BF16)
    partial_sum = jnp.einsum("sn,pna->psa", onehot, inst, preferred_element_type=F32)
    summed = lax.psum_scatter(partial_sum, "grp", scatter_dimension=1, tiled=True)
    return summed.astype(BF16)


def fused_kernel(dom_ref, cnt_ref, slot_ref, d_ref, b_hbm, q_hbm, out_ref,
                 b_v, q_v, tiles, tab_v, tab_s, give, own, rc, sa, sb, ra, rb, sa2, sb2, ra2, rb2, sz, zin, fs, raw, raw_in, raw_s, raw_r,
                 t_sem, b_sem, q_sem, cs, cr, as_, ar, bs, br, as2, ar2, bs2, br2, zs, zr):
    g = lax.axis_index("grp")
    o = lax.axis_index("occ")
    x, y = g % NX, g // NX
    core, z = o % NC, o // NC
    norb, _, _ = b_v.shape
    kdom = dom_ref.shape[0]
    ntiles = slot_ref.shape[1]
    cols, tile = own.shape[2:]
    blocks = tiles.shape[1]
    part_slots = own.shape[1] // (NX * NY)
    slots = part_slots * PARTS
    half = cols // 2
    lo, hi = pl.ds(0, half), pl.ds(half, half)
    to_core = {"grp": g, "occ": z * NC + 1 - core}
    to_x = {"grp": y * NX + 1 - x, "occ": o}
    to_y = {"grp": (1 - y) * NX + x, "occ": o}
    dest = [d for d in (3 - 3 * (z // 2), 2 - z // 2, z + 1 - 2 * (z % 2), z) for _ in range(PARTS)]
    down = [d for d in (z // 2, z // 2, z % 2) for _ in range(PARTS)]
    late = NU - PARTS
    ahead = late - 1
    middle = z % 3

    b_in = [pltpu.make_async_copy(b_hbm.at[i], b_v.at[i], b_sem.at[i]) for i in range(norb)]
    q_in = [pltpu.make_async_copy(q_hbm.at[i], q_v.at[i], q_sem.at[i]) for i in range(norb)]
    for i in range(norb):
        q_in[i].start()
        b_in[i].start()

    barrier = pltpu.get_barrier_semaphore()
    for dev in (to_core, to_x, to_y):
        pl.semaphore_signal(barrier, inc=1, device_id=dev, device_id_type=MESH)

    @pl.when(z > 0)
    def _():
        pl.semaphore_signal(barrier, inc=1, device_id={"grp": g, "occ": o - NC}, device_id_type=MESH)

    @pl.when(z < NZ - 1)
    def _():
        pl.semaphore_signal(barrier, inc=1, device_id={"grp": g, "occ": o + NC}, device_id_type=MESH)

    members = dom_ref.shape[1]
    mine = lax.broadcasted_iota(jnp.int32, (norb, members), 1) == (
        o * norb + lax.broadcasted_iota(jnp.int32, (norb, members), 0))

    def pick(row):
        return jnp.sum(jnp.where(mine, row, 0), axis=1, keepdims=True)

    count = pick(cnt_ref[...])
    wide = (norb, tab_v.shape[1])
    spot = lax.broadcasted_iota(jnp.int32, wide, 1)
    first_tile = lax.broadcasted_iota(jnp.int32, wide, 0) * kdom
    ids = lax.broadcasted_iota(jnp.int32, (norb, ntiles), 1)
    tab = jnp.full(wide, norb * kdom, jnp.int32)
    for k in range(kdom):
        chosen = pick(dom_ref[k : k + 1, :])
        slot = jnp.sum(jnp.where(ids == chosen, slot_ref[...], 0), axis=1, keepdims=True)
        tab = jnp.where((spot == slot) & (count > k), first_tile + k, tab)
    tab_v[...] = tab
    to_smem = pltpu.make_async_copy(tab_v, tab_s, t_sem)
    to_smem.start()
    tiles[norb * kdom] = jnp.zeros(tiles.shape[1:], BF16)

    for i in range(norb):
        q_in[i].wait()
        b_in[i].wait()
        q = q_v[i]
        rows = lax.broadcasted_iota(jnp.int32, q.shape, 0)
        q = jnp.where(rows < count[i : i + 1, :] * tile, q, jnp.zeros_like(q))
        hidden = lax.dot_general(b_v[i], q, (((0,), (0,)), ((), ())), preferred_element_type=F32)
        scaled = (hidden * d_ref[i : i + 1, :]).astype(BF16)
        amp = lax.dot_general(scaled, q, (((1,), (1,)), ((), ())), preferred_element_type=F32)
        for k in range(kdom):
            part = amp[:, k * tile : (k + 1) * tile].astype(BF16)
            tiles[i * kdom + k] = part.reshape(blocks, cols, tile)
    to_smem.wait()
    pl.semaphore_wait(barrier, 4 + (middle + 1) // 2)

    def remote(src, dst, send, recv, dev):
        return pltpu.make_async_remote_copy(
            src_ref=src, dst_ref=dst, send_sem=send, recv_sem=recv, device_id=dev, device_id_type=MESH)

    c0 = [remote(give.at[t], rc.at[t], cs.at[t], cr.at[t], to_core) for t in range(NU)]
    a1 = [remote(sa.at[t], ra.at[t], as_.at[t], ar.at[t], to_x) for t in range(NU)]
    b1 = [remote(sb.at[t], rb.at[t], bs.at[t], br.at[t], to_y) for t in range(NU)]
    a2 = [remote(sa2.at[t], ra2.at[t], as2.at[t], ar2.at[t], to_y) for t in range(NU)]
    b2 = [remote(sb2.at[t], rb2.at[t], bs2.at[t], br2.at[t], to_x) for t in range(NU)]
    zc = []
    for t in range(late):
        to_z = {"grp": g, "occ": (z + 1 - 2 * down[t]) * NC + core}
        lands = dest[t] * PARTS + t % PARTS
        zc.append(remote(sz.at[t], zin.at[down[t], lands], zs.at[t], zr.at[down[t], lands], to_z))

    to_pair = {"grp": g, "occ": (z + 1 - 2 * (z % 2)) * NC + core}
    early = remote(raw, raw_in, raw_s, raw_r, to_pair)

    def gather(t, block, into):
        for q in range(NX * NY):
            @pl.loop(0, part_slots, unroll=4)
            def _(j):
                s = q * slots + (t % PARTS) * part_slots + j
                terms = [tiles[tab_s[i, s], block].astype(F32) for i in range(norb)]
                while len(terms) > 1:
                    terms = [sum(terms[n : n + 2][1:], terms[n]) for n in range(0, len(terms), 2)]
                into[q * part_slots + j] = terms[0].astype(BF16)

    def partner(t):
        gather(t, dest[t] * NC + 1 - core, give.at[t])
        c0[t].start()

    def keep(t):
        gather(t, dest[t] * NC + core, own.at[t])

    def both(t, iy, ix, rows):
        at = pl.ds((iy * NX + ix) * part_slots, part_slots)
        total = own[t, at, rows, :].astype(F32) + rc[t, at, rows, :].astype(F32)
        return total + raw_in[at, rows, :].astype(F32) if t == NU - 1 else total

    def divert(t):
        c0[t].wait_recv()
        for q in range(NX * NY):
            at = pl.ds(q * part_slots, part_slots)
            raw[at] = (own[t, at].astype(F32) + rc[t, at].astype(F32)).astype(BF16)
        early.start()

    def first(t):
        c0[t].wait_recv()
        if t == NU - 1:
            early.wait_recv()
        for j in range(NY):
            sa[t, j] = both(t, j, 1 - x, lo).astype(BF16)
        a1[t].start()
        for j in range(NX):
            sb[t, j] = both(t, 1 - y, j, hi).astype(BF16)
        b1[t].start()

    def second(t):
        a1[t].wait_recv()
        sa2[t] = (both(t, 1 - y, x, lo) + ra[t, 1 - y].astype(F32)).astype(BF16)
        a2[t].start()
        b1[t].wait_recv()
        sb2[t] = (both(t, y, 1 - x, hi) + rb[t, 1 - x].astype(F32)).astype(BF16)
        b2[t].start()

    def plane(t):
        a2[t].wait_recv()
        fs[:, lo, :] = both(t, y, x, lo) + ra[t, y].astype(F32) + ra2[t].astype(F32)
        b2[t].wait_recv()
        fs[:, hi, :] = both(t, y, x, hi) + rb[t, x].astype(F32) + rb2[t].astype(F32)

    def edge(t):
        @pl.when(middle == 0)
        def _():
            plane(t)
            sz[t] = fs[...].astype(BF16)
            zc[t].start()

    def inner(t):
        @pl.when(middle != 0)
        def _():
            plane(t)
            zc[t].wait_recv()
            sz[t] = (fs[...] + zin[down[t], dest[t] * PARTS + t % PARTS].astype(F32)).astype(BF16)
            zc[t].start()

    def landed(t, way):
        at = z * PARTS + t % PARTS
        remote(sz.at[0], zin.at[way, at], zs.at[0], zr.at[way, at], to_core).wait_recv()
        fs[...] += zin[way, at].astype(F32)

    def final(t):
        plane(t)

        @pl.when(z > (1 if t == NU - 1 else 0))
        def _():
            landed(t, 0)

        @pl.when(z < (NZ - 2 if t == NU - 1 else NZ - 1))
        def _():
            landed(t, 1)

        out_ref[pl.ds((t % PARTS) * part_slots, part_slots)] = fs[...].astype(BF16)

    through = [t for t in range(NU) if t != ahead]
    for step in range(len(through) + 1):
        if step < len(through):
            partner(through[step])
            keep(through[step])
            first(through[step])
        if step == 0:
            partner(ahead)
            keep(ahead)
            divert(ahead)
        if step >= 1:
            second(through[step - 1])
        if 0 <= step - 2 < ahead:
            edge(step - 2)
        if 0 <= step - 3 < ahead:
            inner(step - 3)

    @pl.when(middle != 0)
    def _():
        zc[ahead].wait_recv()
        sz[ahead] = zin[down[ahead], dest[ahead] * PARTS + ahead % PARTS]
        zc[ahead].start()

    for t in range(late, NU):
        final(t)

    for t in range(NU):
        c0[t].wait_send()
    for t in through:
        for copy in (a1[t], b1[t], a2[t], b2[t]):
            copy.wait_send()
    for t in range(ahead):
        zc[t].wait_send()
    early.wait_send()

    @pl.when(middle != 0)
    def _():
        zc[ahead].wait_send()


def staged(b_ints, osv_vecs, inv_denom, domains, dom_count, owner_slot):
    norb, rows, naux = b_ints.shape
    nosv = osv_vecs.shape[2]
    members, kdom = domains.shape
    tile = rows // kdom
    ntiles = owner_slot.shape[0]
    blocks = NZ * NC
    cols = naux // blocks
    slots = ntiles // (NX * NY)
    half = cols // 2
    part = slots // PARTS
    quarter = ntiles // PARTS
    lanes = -(-ntiles // 128) * 128
    vm = lambda *shape: pltpu.VMEM(shape, BF16)
    dma = lambda *shape: pltpu.SemaphoreType.DMA(shape)
    in_vmem = pl.BlockSpec(memory_space=pltpu.VMEM)
    summed = pl.pallas_call(
        fused_kernel,
        out_shape=jax.ShapeDtypeStruct((slots, cols, tile), BF16),
        in_specs=[in_vmem] * 4 + [pl.BlockSpec(memory_space=pltpu.HBM)] * 2,
        out_specs=in_vmem,
        scratch_shapes=[
            vm(norb, rows, naux), vm(norb, rows, nosv), vm(norb * kdom + 1, blocks, cols, tile),
            pltpu.VMEM((norb, lanes), jnp.int32), pltpu.SMEM((norb, lanes), jnp.int32),
            vm(NU, quarter, cols, tile), vm(NU, quarter, cols, tile), vm(NU, quarter, cols, tile),
            vm(NU, NY, part, half, tile), vm(NU, NX, part, half, tile),
            vm(NU, NY, part, half, tile), vm(NU, NX, part, half, tile),
            vm(NU, part, half, tile), vm(NU, part, half, tile),
            vm(NU, part, half, tile), vm(NU, part, half, tile),
            vm(NU - PARTS, part, cols, tile), vm(2, NU, part, cols, tile),
            pltpu.VMEM((part, cols, tile), F32), vm(quarter, cols, tile), vm(quarter, cols, tile),
            pltpu.SemaphoreType.DMA, pltpu.SemaphoreType.DMA,
            pltpu.SemaphoreType.DMA, dma(norb), dma(norb),
        ] + [dma(NU)] * 10 + [dma(NU - PARTS), dma(2, NU)],
        compiler_params=pltpu.CompilerParams(
            collective_id=0, has_side_effects=True, vmem_limit_bytes=56 << 20),
        cost_estimate=pl.CostEstimate(
            flops=4 * norb * rows * naux * nosv, bytes_accessed=5 << 20, transcendentals=0),
    )(domains.T, dom_count.reshape(1, members), owner_slot.reshape(1, ntiles), inv_denom, b_ints, osv_vecs)
    return jnp.swapaxes(summed, 0, 1)


def solution(mesh):
    fits = mesh.shape["grp"] == NX * NY and mesh.shape["occ"] == NZ * NC
    return jax.shard_map(
        staged if fits else general,
        mesh=mesh,
        in_specs=(
            P(("grp", "occ"), None, None),
            P(("grp", "occ"), None, None),
            P(("grp", "occ"), None),
            P("grp", None),
            P("grp"),
            P(),
        ),
        out_specs=P("occ", "grp", None),
        check_vma=False,
    )
```

```python
import jax
import jax.numpy as jnp
from jax import lax
from jax.experimental import pallas as pl
from jax.experimental.pallas import tpu as pltpu
from jax.sharding import PartitionSpec as P

MESH = pl.DeviceIdType.MESH
F32 = jnp.float32
BF16 = jnp.bfloat16
NX, NY, NZ, NC = 2, 2, 4, 2


def general(b_ints, osv_vecs, inv_denom, domains, dom_count, owner_slot):
    own = b_ints.shape[0]
    kdom = domains.shape[1]
    tile = b_ints.shape[1] // kdom
    ntiles = owner_slot.shape[0]
    tiles_ids = jnp.arange(ntiles, dtype=jnp.int32)
    keep_all = jnp.arange(kdom, dtype=jnp.int32)[None, :] < dom_count[:, None]
    looked = jnp.sum(jnp.where(domains[:, :, None] == tiles_ids, owner_slot, 0), axis=-1)
    slot_all = jnp.where(keep_all, looked, -1)
    start = lax.axis_index("occ") * own
    keep = lax.dynamic_slice_in_dim(keep_all, start, own, 0)
    rowmask = jnp.repeat(keep, tile, axis=1).astype(BF16)
    masked = b_ints * rowmask[:, :, None]
    hidden = jnp.einsum("ikn,ikp->inp", osv_vecs, masked, preferred_element_type=F32)
    scaled = (hidden * inv_denom[:, :, None]).astype(BF16)
    amp = jnp.einsum("ikn,inp->pik", osv_vecs, scaled, preferred_element_type=F32)
    amp = (amp * rowmask[None].astype(F32)).astype(BF16)
    got = lax.all_to_all(amp, "occ", split_axis=0, concat_axis=1, tiled=True)
    inst = got.reshape(got.shape[0], -1, tile)
    onehot = (slot_all.reshape(-1)[None, :] == tiles_ids[:, None]).astype(BF16)
    partial_sum = jnp.einsum("sn,pna->psa", onehot, inst, preferred_element_type=F32)
    summed = lax.psum_scatter(partial_sum, "grp", scatter_dimension=1, tiled=True)
    return summed.astype(BF16)


def fused_kernel(dom_ref, cnt_ref, slot_ref, d_ref, b_hbm, q_hbm, out_ref,
                 b_v, q_v, tiles, tab_v, tab_s, give, own, rc, sa, sb, ra, rb, sa2, sb2, ra2, rb2, sz, zin, fs,
                 t_sem, b_sem, q_sem, cs, cr, as_, ar, bs, br, as2, ar2, bs2, br2, zs, zr):
    g = lax.axis_index("grp")
    o = lax.axis_index("occ")
    x, y = g % NX, g // NX
    core, z = o % NC, o // NC
    norb, _, _ = b_v.shape
    kdom = dom_ref.shape[0]
    ntiles, cols, tile = own.shape[1:]
    blocks = tiles.shape[1]
    slots = ntiles // (NX * NY)
    half = cols // 2
    lo, hi = pl.ds(0, half), pl.ds(half, half)
    to_core = {"grp": g, "occ": z * NC + 1 - core}
    to_x = {"grp": y * NX + 1 - x, "occ": o}
    to_y = {"grp": (1 - y) * NX + x, "occ": o}
    dest = [3 - 3 * (z // 2), (2 + 3 * z) % 5, 1 + z % 2, z]
    down = [z // 2, z % 2, z // 2]
    middle = z % 3

    b_in = [pltpu.make_async_copy(b_hbm.at[i], b_v.at[i], b_sem.at[i]) for i in range(norb)]
    q_in = [pltpu.make_async_copy(q_hbm.at[i], q_v.at[i], q_sem.at[i]) for i in range(norb)]
    for i in range(norb):
        q_in[i].start()
        b_in[i].start()

    barrier = pltpu.get_barrier_semaphore()
    for dev in (to_core, to_x, to_y):
        pl.semaphore_signal(barrier, inc=1, device_id=dev, device_id_type=MESH)

    @pl.when(z > 0)
    def _():
        pl.semaphore_signal(barrier, inc=1, device_id={"grp": g, "occ": o - NC}, device_id_type=MESH)

    @pl.when(z < NZ - 1)
    def _():
        pl.semaphore_signal(barrier, inc=1, device_id={"grp": g, "occ": o + NC}, device_id_type=MESH)

    members = dom_ref.shape[1]
    mine = lax.broadcasted_iota(jnp.int32, (norb, members), 1) == (
        o * norb + lax.broadcasted_iota(jnp.int32, (norb, members), 0))

    def pick(row):
        return jnp.sum(jnp.where(mine, row, 0), axis=1, keepdims=True)

    count = pick(cnt_ref[...])
    wide = (norb, tab_v.shape[1])
    spot = lax.broadcasted_iota(jnp.int32, wide, 1)
    first_tile = lax.broadcasted_iota(jnp.int32, wide, 0) * kdom
    ids = lax.broadcasted_iota(jnp.int32, (norb, ntiles), 1)
    tab = jnp.full(wide, norb * kdom, jnp.int32)
    for k in range(kdom):
        chosen = pick(dom_ref[k : k + 1, :])
        slot = jnp.sum(jnp.where(ids == chosen, slot_ref[...], 0), axis=1, keepdims=True)
        tab = jnp.where((spot == slot) & (count > k), first_tile + k, tab)
    tab_v[...] = tab
    to_smem = pltpu.make_async_copy(tab_v, tab_s, t_sem)
    to_smem.start()
    tiles[norb * kdom] = jnp.zeros(tiles.shape[1:], BF16)

    for i in range(norb):
        q_in[i].wait()
        b_in[i].wait()
        q = q_v[i]
        rows = lax.broadcasted_iota(jnp.int32, q.shape, 0)
        q = jnp.where(rows < count[i : i + 1, :] * tile, q, jnp.zeros_like(q))
        hidden = lax.dot_general(b_v[i], q, (((0,), (0,)), ((), ())), preferred_element_type=F32)
        scaled = (hidden * d_ref[i : i + 1, :]).astype(BF16)
        amp = lax.dot_general(scaled, q, (((1,), (1,)), ((), ())), preferred_element_type=F32)
        for k in range(kdom):
            part = amp[:, k * tile : (k + 1) * tile].astype(BF16)
            tiles[i * kdom + k] = part.reshape(blocks, cols, tile)
    to_smem.wait()
    pl.semaphore_wait(barrier, 4 + (middle + 1) // 2)

    def remote(src, dst, send, recv, dev):
        return pltpu.make_async_remote_copy(
            src_ref=src, dst_ref=dst, send_sem=send, recv_sem=recv, device_id=dev, device_id_type=MESH)

    c0 = [remote(give.at[t], rc.at[t], cs.at[t], cr.at[t], to_core) for t in range(NZ)]
    a1 = [remote(sa.at[t], ra.at[t], as_.at[t], ar.at[t], to_x) for t in range(NZ)]
    b1 = [remote(sb.at[t], rb.at[t], bs.at[t], br.at[t], to_y) for t in range(NZ)]
    a2 = [remote(sa2.at[t], ra2.at[t], as2.at[t], ar2.at[t], to_y) for t in range(NZ)]
    b2 = [remote(sb2.at[t], rb2.at[t], bs2.at[t], br2.at[t], to_x) for t in range(NZ)]
    zc = []
    for t in range(NZ - 1):
        to_z = {"grp": g, "occ": (z + 1 - 2 * down[t]) * NC + core}
        zc.append(remote(sz.at[t], zin.at[down[t], dest[t]], zs.at[t], zr.at[down[t], dest[t]], to_z))

    def gather(*pairs):
        @pl.loop(0, ntiles, unroll=4)
        def _(s):
            picks = [tab_s[i, s] for i in range(norb)]
            for block, into in pairs:
                terms = [tiles[pick_i, block].astype(F32) for pick_i in picks]
                while len(terms) > 1:
                    terms = [sum(terms[j : j + 2][1:], terms[j]) for j in range(0, len(terms), 2)]
                into[s] = terms[0].astype(BF16)

    def partner(t):
        theirs = (dest[t] * NC + 1 - core, give.at[t])
        ours = (dest[t] * NC + core, own.at[t])
        if t == 0:
            gather(theirs)
            c0[t].start()
            gather(ours)
        else:
            gather(theirs, ours)
            c0[t].start()

    def both(t, iy, ix, rows):
        at = pl.ds((iy * NX + ix) * slots, slots)
        return own[t, at, rows, :].astype(F32) + rc[t, at, rows, :].astype(F32)

    def first(t):
        c0[t].wait_recv()
        for j in range(NY):
            sa[t, j] = both(t, j, 1 - x, lo).astype(BF16)
        a1[t].start()
        for j in range(NX):
            sb[t, j] = both(t, 1 - y, j, hi).astype(BF16)
        b1[t].start()

    def second(t):
        a1[t].wait_recv()
        sa2[t] = (both(t, 1 - y, x, lo) + ra[t, 1 - y].astype(F32)).astype(BF16)
        a2[t].start()
        b1[t].wait_recv()
        sb2[t] = (both(t, y, 1 - x, hi) + rb[t, 1 - x].astype(F32)).astype(BF16)
        b2[t].start()

    def plane(t):
        a2[t].wait_recv()
        fs[:, lo, :] = both(t, y, x, lo) + ra[t, y].astype(F32) + ra2[t].astype(F32)
        b2[t].wait_recv()
        fs[:, hi, :] = both(t, y, x, hi) + rb[t, x].astype(F32) + rb2[t].astype(F32)

    def edge(t):
        @pl.when(middle == 0)
        def _():
            plane(t)
            sz[t] = fs[...].astype(BF16)
            zc[t].start()

    def inner(t):
        @pl.when(middle != 0)
        def _():
            plane(t)
            zc[t].wait_recv()
            sz[t] = (fs[...] + zin[down[t], dest[t]].astype(F32)).astype(BF16)
            zc[t].start()

    partner(0)
    first(0)
    partner(1)
    first(1)
    second(0)
    partner(2)
    first(2)
    second(1)
    edge(0)
    partner(3)
    first(3)
    second(2)
    inner(0)
    edge(1)
    second(3)
    inner(1)
    edge(2)
    inner(2)
    plane(3)

    def landed(way):
        remote(sz.at[0], zin.at[way, z], zs.at[0], zr.at[way, z], to_core).wait_recv()
        fs[...] += zin[way, z].astype(F32)

    @pl.when(z > 0)
    def _():
        landed(0)

    @pl.when(z < NZ - 1)
    def _():
        landed(1)

    out_ref[...] = fs[...].astype(BF16)
    for t in range(NZ):
        for copy in (c0[t], a1[t], b1[t], a2[t], b2[t]):
            copy.wait_send()
    for t in range(NZ - 1):
        zc[t].wait_send()


def staged(b_ints, osv_vecs, inv_denom, domains, dom_count, owner_slot):
    norb, rows, naux = b_ints.shape
    nosv = osv_vecs.shape[2]
    members, kdom = domains.shape
    tile = rows // kdom
    ntiles = owner_slot.shape[0]
    blocks = NZ * NC
    cols = naux // blocks
    slots = ntiles // (NX * NY)
    half = cols // 2
    lanes = -(-ntiles // 128) * 128
    vm = lambda *shape: pltpu.VMEM(shape, BF16)
    dma = lambda *shape: pltpu.SemaphoreType.DMA(shape)
    in_vmem = pl.BlockSpec(memory_space=pltpu.VMEM)
    summed = pl.pallas_call(
        fused_kernel,
        out_shape=jax.ShapeDtypeStruct((slots, cols, tile), BF16),
        in_specs=[in_vmem] * 4 + [pl.BlockSpec(memory_space=pl.ANY)] * 2,
        out_specs=in_vmem,
        scratch_shapes=[
            vm(norb, rows, naux), vm(norb, rows, nosv), vm(norb * kdom + 1, blocks, cols, tile),
            pltpu.VMEM((norb, lanes), jnp.int32), pltpu.SMEM((norb, lanes), jnp.int32),
            vm(NZ, ntiles, cols, tile), vm(NZ, ntiles, cols, tile), vm(NZ, ntiles, cols, tile),
            vm(NZ, NY, slots, half, tile), vm(NZ, NX, slots, half, tile),
            vm(NZ, NY, slots, half, tile), vm(NZ, NX, slots, half, tile),
            vm(NZ, slots, half, tile), vm(NZ, slots, half, tile),
            vm(NZ, slots, half, tile), vm(NZ, slots, half, tile),
            vm(NZ - 1, slots, cols, tile), vm(2, NZ, slots, cols, tile),
            pltpu.VMEM((slots, cols, tile), F32),
            pltpu.SemaphoreType.DMA, dma(norb), dma(norb),
        ] + [dma(NZ)] * 10 + [dma(NZ - 1), dma(2, NZ)],
        compiler_params=pltpu.CompilerParams(
            collective_id=0, has_side_effects=True, vmem_limit_bytes=56 << 20),
        cost_estimate=pl.CostEstimate(
            flops=4 * norb * rows * naux * nosv, bytes_accessed=5 << 20, transcendentals=0),
    )(domains.T, dom_count.reshape(1, members), owner_slot.reshape(1, ntiles), inv_denom, b_ints, osv_vecs)
    return jnp.swapaxes(summed, 0, 1)


def solution(mesh):
    fits = mesh.shape["grp"] == NX * NY and mesh.shape["occ"] == NZ * NC
    return jax.shard_map(
        staged if fits else general,
        mesh=mesh,
        in_specs=(
            P(("grp", "occ"), None, None),
            P(("grp", "occ"), None, None),
            P(("grp", "occ"), None),
            P("grp", None),
            P("grp"),
            P(),
        ),
        out_specs=P("occ", "grp", None),
        check_vma=False,
    )
```
